512 devices in a mesh: img: 64 (over z_hi, x, y), tp: 8 (over z_lo, core).
Axes of the slice: x: 4, y: 8, z: 8 (z_hi: 2, z_lo: 4; z = z_hi * 4 + z_lo), core: 2. Of those that a mesh axis runs over, the one named last changes fastest.
Arguments:
- vit_hidden: bfloat16 [8192, 6400], P('img', 'tp'), may hold values from -6 to 6
- residual_stream: bfloat16 [8192, 3200], P('img'), may hold values from -6 to 6
- fc2_weight: bfloat16 [6400, 3200], P('tp', 'img'), may hold values from -0.078125 to 0.078125
- ln_gain: float32 [3200], replicated, may hold values from 0.1 to 1.9
- key_weight: bfloat16 [3200, 2048], P('img', 'tp'), may hold values from -0.109375 to 0.109375
- value_weight: bfloat16 [3200, 2048], P('img', 'tp'), may hold values from -0.109375 to 0.109375
- query_heads: bfloat16 [96, 2048], P(None, 'tp'), may hold values from -64 to 64
- dest_shard: int32 [64], P('img'), may hold values from 0 to 63, as said below
- row_offset: int32 [64], P('img'), may hold values from 0 to 288, as said below
Outputs:
- llm_rows: bfloat16 [24576, 2048], P('img', 'tp')
The draws below stay inside these ranges and needn't reach their ends.
Inputs may be any that keep to these rules, and one draw needn't show every extreme that they name: `dest_shard`: image slots of one shard never intersect; some shard holds 4 images in every draw. `row_offset`: a multiple of 96.
All inputs are finite; a program needn't handle non-finite values.
Results may differ from the reference program's by a relative error of at most 0.039.
Values may be sent and summed in bfloat16 or wider, within the bound.
A program may use at most 64 MiB of HBM per device.

```python
import jax
import jax.numpy as jnp
from jax import lax

VIT_W = 3200
VIT_FF = 6400
HEAD_DIM = 128
HEADS = 16
QUERIES = 96
MOST_IMG = 4
PATCHES = 128
IMAGES = 64
ROWS = 8192
RES_W = 2048
SHARD_ROWS = 384
N_TP = 8


def packing_slots(key):
    count = IMAGES * MOST_IMG
    order = jax.random.permutation(key, count)
    ranks = jnp.argsort(order).astype(jnp.int32)
    chosen = jax.random.randint(jax.random.fold_in(key, 11), (), 0, IMAGES).astype(jnp.int32)
    slot = jnp.arange(count, dtype=jnp.int32)
    score = jnp.where(slot // MOST_IMG == chosen, count + slot, ranks)
    others = jnp.argsort(score, stable=True)[:IMAGES - MOST_IMG].astype(jnp.int32)
    mixing = jax.random.permutation(jax.random.fold_in(key, 13), IMAGES - MOST_IMG).astype(jnp.int32)
    image = jnp.arange(IMAGES, dtype=jnp.int32)
    rot = (image - chosen - IMAGES // 2) % IMAGES
    forced = chosen * MOST_IMG + jnp.minimum(rot, MOST_IMG - 1)
    rest = others[mixing[jnp.clip(rot - MOST_IMG, 0, IMAGES - MOST_IMG - 1)]]
    return jnp.where(rot < MOST_IMG, forced, rest).astype(jnp.int32)


def draw_dest_shard(key, part):
    picked = packing_slots(key)
    return (picked // MOST_IMG).astype(jnp.int32)


def draw_row_offset(key, part):
    picked = packing_slots(key)
    return (picked % MOST_IMG * QUERIES).astype(jnp.int32)


def draw_query_heads(key, part):
    key = jax.random.fold_in(key, 3)
    base = jnp.clip(jax.random.normal(key, (QUERIES, RES_W), jnp.float32), -6.0, 6.0)
    return base.astype(jnp.bfloat16)


def block_scale(stream_key, extent, split, least, high):
    factor_of = 1.0
    for dim, blocks in split:
        steps = jax.random.uniform(jax.random.fold_in(jax.random.fold_in(stream_key, 6), dim), (blocks,), jnp.float32, least / len(split), high / len(split))
        factor_of = factor_of * jnp.repeat(jnp.exp(steps), extent[dim] // blocks).reshape((-1,) + (1,) * (len(extent) - 1 - dim))
    return factor_of


def normal_values(rng, extent, width, most, cuts=(), kind=jnp.bfloat16):
    entries = jax.random.normal(rng, extent, jnp.float32) * width
    if len(cuts) > 0:
        entries = block_scale(rng, extent, cuts, -0.22, 0.18) * entries
    return jnp.clip(entries, min=-most, max=most).astype(kind)


def setup_inputs(seed: int = 0) -> dict:
    key_of = jax.random.split(jax.random.key(seed), 10)
    return {
        "vit_hidden": normal_values(key_of[0], (ROWS, VIT_FF), 1.0, 6.0, ((0, 64), (1, 8))),
        "residual_stream": normal_values(key_of[1], (ROWS, VIT_W), 1.0, 6.0, ((0, 64),)),
        "fc2_weight": normal_values(key_of[2], (VIT_FF, VIT_W), VIT_FF ** -0.5, 0.078125, ((0, 8), (1, 64))),
        "ln_gain": jnp.clip(1.0 + 0.18 * jax.random.normal(key_of[3], (VIT_W,), jnp.float32), 0.1, 1.9),
        "key_weight": normal_values(key_of[4], (VIT_W, RES_W), VIT_W ** -0.5, 0.109375, ((0, 64), (1, 8))),
        "value_weight": normal_values(key_of[5], (VIT_W, RES_W), VIT_W ** -0.5, 0.109375, ((0, 64), (1, 8))),
        "query_heads": draw_query_heads(jax.random.fold_in(key_of[9], 71), 0),
        "dest_shard": draw_dest_shard(jax.random.fold_in(key_of[9], 71), 0),
        "row_offset": draw_row_offset(jax.random.fold_in(key_of[9], 71), 0),
    }


def reference(vit_hidden, residual_stream, fc2_weight, ln_gain, key_weight, value_weight, query_heads, dest_shard, row_offset):
    block = VIT_FF // N_TP
    total = jnp.zeros((ROWS, VIT_W), jnp.float32)
    for t in range(N_TP):
        act = jax.nn.gelu(vit_hidden[:, t * block:(t + 1) * block].astype(jnp.float32)).astype(jnp.bfloat16)
        part = jnp.dot(act, fc2_weight[t * block:(t + 1) * block], preferred_element_type=jnp.float32).astype(jnp.bfloat16)
        part = lax.optimization_barrier(part)
        total = total + part.astype(jnp.float32)
    stream = residual_stream.astype(jnp.float32) + total
    mean = lax.optimization_barrier(jnp.mean(stream, axis=1, keepdims=True))
    var = lax.optimization_barrier(jnp.mean(stream * stream, axis=1, keepdims=True)) - mean * mean
    normed = ((stream - mean) * lax.rsqrt(var + 1e-06) * ln_gain).astype(jnp.bfloat16)
    keys = jnp.dot(normed, key_weight, preferred_element_type=jnp.float32).astype(jnp.bfloat16)
    values = jnp.dot(normed, value_weight, preferred_element_type=jnp.float32).astype(jnp.bfloat16)
    keys = keys.reshape(IMAGES, PATCHES, HEADS, HEAD_DIM)
    values = values.reshape(IMAGES, PATCHES, HEADS, HEAD_DIM)
    queries = query_heads.reshape(QUERIES, HEADS, HEAD_DIM).astype(jnp.float32)
    scale = 1.0 / HEAD_DIM ** 0.5

    def attend(pair):
        kimg, vimg = pair
        scores = jnp.einsum('qhd,phd->hqp', queries, kimg.astype(jnp.float32)) * scale
        peak = lax.optimization_barrier(jnp.max(scores, axis=2, keepdims=True))
        expo = jnp.exp(scores - peak)
        weights = (expo / lax.optimization_barrier(jnp.sum(expo, axis=2, keepdims=True))).astype(jnp.bfloat16)
        mixed = jnp.einsum('hqp,phd->qhd', weights.astype(jnp.float32), vimg.astype(jnp.float32))
        return mixed.astype(jnp.bfloat16).reshape(QUERIES, RES_W)
    resampled = lax.map(attend, (keys, values))
    index = ((dest_shard * SHARD_ROWS + row_offset)[:, None] + jnp.arange(QUERIES, dtype=jnp.int32)[None, :]).reshape(-1).astype(jnp.int32)
    output = jnp.zeros((IMAGES * SHARD_ROWS, RES_W), jnp.bfloat16)
    return output.at[index].set(resampled.reshape(IMAGES * QUERIES, RES_W))
```

```python
import functools

import jax
import jax.numpy as jnp
from jax import lax
from jax.experimental import pallas as pl
from jax.experimental.pallas import tpu as pltpu
from jax.sharding import PartitionSpec as P

HEAD_DIM = 128
MOST_IMG = 4
ZH, X, Y, ZL, CORES = 2, 4, 8, 4, 2
EPS = 1e-06
MESH = pl.DeviceIdType.MESH
F32 = jnp.float32
BF16 = jnp.bfloat16
COPIES = 96


def window(base, align, span):
    start = lax.div(base, align) * align
    return pl.multiple_of(start, align), base - start


def kernel(
    hidden_ref,
    res_ref,
    w_ref,
    gain_ref,
    kw_ref,
    vw_ref,
    q_ref,
    dest_ref,
    off_ref,
    out_ref,
    act,
    wl,
    kvl,
    own32,
    meta,
    w32,
    kv32,
    res_t,
    res_in,
    resid,
    gain_t,
    part_f,
    part_b,
    part_x,
    half_f,
    half_b,
    half_r,
    stats,
    normed,
    kv_s,
    kv_r,
    rows,
    slab,
    slab_r,
    ss,
    rs,
):
    depth, patches = hidden_ref.shape
    cw = w_ref.shape[0]
    width = res_ref.shape[1]
    kvw = kw_ref.shape[1]
    nquery = q_ref.shape[0]
    heads = kvw // HEAD_DIM
    group = Y * cw

    img = lax.axis_index("img")
    tp = lax.axis_index("tp")
    zh = lax.div(img, X * Y)
    x = lax.rem(lax.div(img, Y), X)
    y = lax.rem(img, Y)
    zl = lax.div(tp, CORES)
    c = lax.rem(tp, CORES)

    def dev(dzh=0, dx=0, dy=0, dzl=0, dc=0):
        a = lax.rem(zh + dzh, ZH)
        b = lax.rem(x + dx + X, X)
        d = lax.rem(y + dy + Y, Y)
        e = lax.rem(zl + dzl + ZL, ZL)
        f = lax.rem(c + dc, CORES)
        return ((a * X + b) * Y + d, e * CORES + f)

    used = [0]
    pending = []

    def copy(src, dst, device):
        n = used[0]
        used[0] += 1
        assert n < COPIES
        return pltpu.make_async_remote_copy(
            src_ref=src,
            dst_ref=dst,
            send_sem=ss.at[n],
            recv_sem=rs.at[n],
            device_id=device,
            device_id_type=MESH,
        )

    def send(src, dst, device):
        cp = copy(src, dst, device)
        cp.start()
        pending.append(cp)
        return cp

    partners = (
        [dev(dzh=1)]
        + [dev(dy=d) for d in range(1, Y)]
        + [dev(dx=d) for d in range(1, X)]
        + [dev(dzl=d) for d in range(1, ZL)]
        + [dev(dc=1)]
        + [dev(dx=d, dzl=-d, dc=k) for d in range(1, X) for k in range(CORES)]
    )
    barrier = pltpu.get_barrier_semaphore()
    for partner in partners:
        pl.semaphore_signal(barrier, inc=1, device_id=partner, device_id_type=MESH)

    own32[0:cw, :] = w_ref[...].astype(F32)
    own32[cw : cw + 1, :] = jnp.full((1, depth), dest_ref[0].astype(F32), F32)
    own32[cw + 1 : cw + 2, :] = jnp.full((1, depth), off_ref[0].astype(F32), F32)
    wl[0, 0] = own32[...].astype(BF16)
    kvl[0, 0, :, 0:kvw] = kw_ref[...]
    kvl[0, 0, :, kvw : 2 * kvw] = vw_ref[...]
    act[0] = jax.nn.gelu(hidden_ref[...].astype(F32)).astype(BF16)
    pl.semaphore_wait(barrier, len(partners))

    w_zh = send(wl.at[0, 0], wl.at[1, 0], dev(dzh=1))
    right, left = {}, {}
    right[0, 1] = send(wl.at[0, 0], wl.at[0, Y - 1], dev(dy=1))
    left[0, 1] = send(wl.at[0, 0], wl.at[0, 1], dev(dy=-1))
    kv_zh = send(kvl.at[0, 0], kvl.at[1, 0], dev(dzh=1))
    act_x = [send(act.at[0], act.at[X - d], dev(dx=d)) for d in range(1, X)]

    owner_x = lax.rem(x - zl + X, X)
    start, shift = window((lax.rem(zh + c, ZH) * X + owner_x) * group, 128, 512)
    res_t[...] = res_ref[:, pl.ds(start, 512)].astype(F32).T.astype(BF16)
    shift = pl.multiple_of(shift, 16)
    res_cp = copy(res_t.at[pl.ds(shift, group)], res_in, dev(dx=-zl))

    @pl.when(zl != 0)
    def _():
        res_cp.start()

    @pl.when(zl == 0)
    def _():
        res_in[...] = res_t[pl.ds(shift, group), :]

    w_zh.wait_recv()
    right[1, 1] = send(wl.at[1, 0], wl.at[1, Y - 1], dev(dy=1))
    left[1, 1] = send(wl.at[1, 0], wl.at[1, 1], dev(dy=-1))

    turn = lax.rem(group - cw * y, group)
    start_g, shift_g = window((lax.rem(zh + c, ZH) * X + x) * group, 128, 512)
    gain_t[...] = jnp.broadcast_to(gain_ref[:, pl.ds(start_g, 512)], (128, 512)).T
    gain_col = pltpu.roll(gain_t[pl.ds(pl.multiple_of(shift_g, 16), group), :], turn, 0)
    gain_t[0:group, :] = gain_col

    def pack(h, r):
        block = wl[h, r].astype(F32)
        w32[h, r * cw : r * cw + cw, :] = block[0:cw, :]
        top = cw // 8 * 8
        meta[h * Y + r, 0 : cw + 2 - top, :] = block[top : cw + 2, 0:kvw]

    pack(0, 0)
    pack(1, 0)
    for s in range(1, Y // 2):
        for h in range(ZH):
            right[h, s].wait_recv()
            if s < Y // 2 - 1 or h == 0:
                right[h, s + 1] = send(wl.at[h, Y - s], wl.at[h, Y - s - 1], dev(dy=1))
            left[h, s].wait_recv()
            if s < Y // 2 - 1 or h == 1:
                left[h, s + 1] = send(wl.at[h, s], wl.at[h, s + 1], dev(dy=-1))
            pack(h, Y - s)
            pack(h, s)
    right[0, Y // 2].wait_recv()
    pack(0, Y // 2)
    left[1, Y // 2].wait_recv()
    pack(1, Y // 2)

    kv_zh.wait_recv()
    kv_y = [
        send(kvl.at[h, 0], kvl.at[h, Y - d], dev(dy=d)) for h in range(ZH) for d in range(1, Y)
    ]

    for cp in act_x:
        cp.wait_recv()
    acts = jnp.concatenate([act[k] for k in range(X)], axis=1)
    for h in range(ZH):
        p = jnp.dot(w32[h].astype(BF16), acts, preferred_element_type=F32)
        part_f[h] = p
        part_b[h] = p.astype(BF16)
    core_cp = send(part_b.at[1 - c], part_x, dev(dc=1))
    core_cp.wait_recv()
    mine = part_f[c] + part_x[...].astype(F32)
    for k in range(X):
        blk = mine[:, k * patches : (k + 1) * patches]
        half_f[k] = blk
        half_b[k] = blk.astype(BF16)
    sums = [
        send(half_b.at[lax.rem(zl + d, ZL)], half_r.at[d - 1], dev(dzl=d)) for d in range(1, ZL)
    ]

    @pl.when(zl != 0)
    def _():
        res_cp.wait_recv()

    resid[...] = pltpu.roll(res_in[...].astype(F32), turn, 0)
    total = half_f[zl] + resid[...]
    for d in range(1, ZL):
        sums[d - 1].wait_recv()
        total = total + half_r[d - 1].astype(F32)

    tall = total.reshape(group // 8, 8, patches)
    stats[0, 0:8] = jnp.sum(tall, axis=0)
    stats[0, 8:16] = jnp.sum(tall * tall, axis=0)
    st = []
    for d in range(X):
        for k in range(CORES):
            if d or k:
                st.append(send(stats.at[0], stats.at[d * CORES + k], dev(dx=d, dzl=-d, dc=k)))
    for cp in st:
        cp.wait_recv()
    both = jnp.sum(stats[...], axis=0)
    mean = jnp.sum(both[0:8], axis=0, keepdims=True) / width
    var = jnp.sum(both[8:16], axis=0, keepdims=True) / width - mean * mean
    normed[c, zl] = ((total - mean) * lax.rsqrt(var + EPS) * gain_t[0:group, :]).astype(BF16)

    ag = [send(normed.at[c, zl], normed.at[c, zl], dev(dzl=d)) for d in range(1, ZL)]
    fw = [send(normed.at[c, zl], normed.at[c, zl], dev(dc=1))]

    for cp in kv_y:
        cp.wait_recv()
    for h in range(ZH):
        for r in range(Y):
            kv32[h, r * cw : r * cw + cw, :] = kvl[h, r].astype(F32)

    for d in range(1, ZL):
        ag[d - 1].wait_recv()
        slot = normed.at[c, lax.rem(zl - d + ZL, ZL)]
        fw.append(send(slot, slot, dev(dc=1)))
    for cp in fw:
        cp.wait_recv()

    acc = None
    for h in range(ZH):
        nt = jnp.concatenate([normed[h, k] for k in range(X)], axis=1)
        p = lax.dot_general(
            kv32[h].astype(BF16), nt, (((0,), (0,)), ((), ())), preferred_element_type=F32
        )
        acc = p if acc is None else acc + p
    for d in range(1, X):
        kv_s[d - 1] = acc[:, d * patches : (d + 1) * patches].astype(BF16)
    kvs = [send(kv_s.at[d - 1], kv_r.at[d - 1], dev(dx=d)) for d in range(1, X)]
    kv = acc[:, 0:patches]
    for d in range(1, X):
        kvs[d - 1].wait_recv()
        kv = kv + kv_r[d - 1].astype(F32)
    kv = kv.astype(BF16)

    for n in range(heads):
        lanes = slice(n * HEAD_DIM, (n + 1) * HEAD_DIM)
        kt = kv[n * HEAD_DIM : (n + 1) * HEAD_DIM, :]
        vt = kv[kvw + n * HEAD_DIM : kvw + (n + 1) * HEAD_DIM, :]
        scores = jnp.dot(q_ref[:, lanes], kt, preferred_element_type=F32) * (1.0 / HEAD_DIM**0.5)
        expo = jnp.exp(scores - jnp.max(scores, axis=1, keepdims=True))
        weights = (expo / jnp.sum(expo, axis=1, keepdims=True)).astype(BF16)
        mixed = lax.dot_general(
            weights, vt, (((1,), (1,)), ((), ())), preferred_element_type=F32
        )
        rows[0, 0, :, lanes] = mixed.astype(BF16)

    r_zh = send(rows.at[0, 0], rows.at[1, 0], dev(dzh=1))
    got = [send(rows.at[0, 0], rows.at[0, Y - d], dev(dy=d)) for d in range(1, Y)]
    r_zh.wait_recv()
    got += [send(rows.at[1, 0], rows.at[1, Y - d], dev(dy=d)) for d in range(1, Y)]
    for cp in got:
        cp.wait_recv()

    skip = cw - cw // 8 * 8
    for k in range(X):
        shard = ((zh * X + lax.rem(x + k, X)) * Y + y).astype(F32)
        for s in range(MOST_IMG):
            picked = None
            for n in range(ZH * Y):
                here = (meta[n, skip : skip + 1, :] == shard) & (
                    meta[n, skip + 1 : skip + 2, :] == float(s * nquery)
                )
                term = rows[n // Y, n % Y] * jnp.where(here, 1.0, 0.0).astype(BF16)
                picked = term if picked is None else picked + term
            slab[k, s * nquery : (s + 1) * nquery, :] = picked
    slabs = [send(slab.at[d], slab_r.at[d - 1], dev(dx=d)) for d in range(1, X)]
    result = slab[0]
    for d in range(1, X):
        slabs[d - 1].wait_recv()
        result = result + slab_r[d - 1]
    out_ref[...] = result

    @pl.when(zl != 0)
    def _():
        res_cp.wait_send()

    for cp in pending:
        cp.wait_send()


def local(
    vit_hidden,
    residual_stream,
    fc2_weight,
    ln_gain,
    key_weight,
    value_weight,
    query_heads,
    dest_shard,
    row_offset,
):
    patches, depth = vit_hidden.shape
    cw = fc2_weight.shape[1]
    kvw = key_weight.shape[1]
    nquery = query_heads.shape[0]
    width = residual_stream.shape[1]
    group = Y * cw
    shard_rows = MOST_IMG * nquery
    vmem = pl.BlockSpec(memory_space=pltpu.VMEM)
    smem = pl.BlockSpec(memory_space=pltpu.SMEM)
    return pl.pallas_call(
        kernel,
        out_shape=jax.ShapeDtypeStruct((shard_rows, kvw), BF16),
        in_specs=[vmem] * 7 + [smem] * 2,
        out_specs=vmem,
        scratch_shapes=[
            pltpu.VMEM((X, depth, patches), BF16),
            pltpu.VMEM((ZH, Y, cw + 2, depth), BF16),
            pltpu.VMEM((ZH, Y, cw, 2 * kvw), BF16),
            pltpu.VMEM((cw + 2, depth), F32),
            pltpu.VMEM((ZH * Y, 8, kvw), F32),
            pltpu.VMEM((ZH, group, depth), F32),
            pltpu.VMEM((ZH, group, 2 * kvw), F32),
            pltpu.VMEM((512, 128), BF16),
            pltpu.VMEM((group, patches), BF16),
            pltpu.VMEM((group, patches), F32),
            pltpu.VMEM((512, 128), F32),
            pltpu.VMEM((ZH, group, X * patches), F32),
            pltpu.VMEM((ZH, group, X * patches), BF16),
            pltpu.VMEM((group, X * patches), BF16),
            pltpu.VMEM((X, group, patches), F32),
            pltpu.VMEM((X, group, patches), BF16),
            pltpu.VMEM((ZL - 1, group, patches), BF16),
            pltpu.VMEM((X * CORES, 16, patches), F32),
            pltpu.VMEM((ZH, X, group, patches), BF16),
            pltpu.VMEM((X - 1, 2 * kvw, patches), BF16),
            pltpu.VMEM((X - 1, 2 * kvw, patches), BF16),
            pltpu.VMEM((ZH, Y, nquery, kvw), BF16),
            pltpu.VMEM((X, shard_rows, kvw), BF16),
            pltpu.VMEM((X - 1, shard_rows, kvw), BF16),
            pltpu.SemaphoreType.DMA((COPIES,)),
            pltpu.SemaphoreType.DMA((COPIES,)),
        ],
        compiler_params=pltpu.CompilerParams(
            collective_id=0, has_side_effects=True, vmem_limit_bytes=48 * 2**20
        ),
        cost_estimate=pl.CostEstimate(
            flops=1100000000, bytes_accessed=3000000, transcendentals=200000
        ),
        name="encoder_resampler",
    )(
        vit_hidden.T,
        residual_stream,
        fc2_weight.T,
        ln_gain.reshape(1, width),
        key_weight,
        value_weight,
        query_heads,
        dest_shard,
        row_offset,
    )


def solution(mesh):
    return jax.shard_map(
        local,
        mesh=mesh,
        in_specs=(
            P("img", "tp"),
            P("img", None),
            P("tp", "img"),
            P(),
            P("img", "tp"),
            P("img", "tp"),
            P(None, "tp"),
            P("img"),
            P("img"),
        ),
        out_specs=P("img", "tp"),
        check_vma=False,
    )
```

```python
import functools

import jax
import jax.numpy as jnp
from jax import lax
from jax.experimental import pallas as pl
from jax.experimental.pallas import tpu as pltpu
from jax.sharding import PartitionSpec as P

HEAD_DIM = 128
MOST_IMG = 4
ZH, X, Y, ZL, CORES = 2, 4, 8, 4, 2
EPS = 1e-06
MESH = pl.DeviceIdType.MESH
F32 = jnp.float32
BF16 = jnp.bfloat16
COPIES = 160
ARRIVAL = (0, 1, 7, 2, 6, 3, 5, 4)
FAR_Y = (4, 3, 5, 2, 6, 1, 7)
FAR_X = (2, 1, 3)


def window(base, align):
    start = lax.div(base, align) * align
    return pl.multiple_of(start, align), base - start


def kernel(
    hidden_ref,
    res_ref,
    w_ref,
    gain_ref,
    kw_ref,
    vw_ref,
    q_ref,
    dest_ref,
    off_ref,
    out_ref,
    act,
    wl_a,
    wl_b,
    kvl,
    own32,
    meta,
    w32,
    kv32,
    res_t,
    res_in,
    turned,
    resid,
    gain_t,
    part_f,
    part_b,
    part_x,
    half_f,
    half_b,
    half_r,
    stats,
    normed,
    kv_s,
    kv_r,
    rows,
    slab,
    slab_r,
    ss,
    rs,
    ls,
    hidden_v,
    res_v,
    w_v,
    gain_v,
    q_v,
):
    depth, patches = hidden_ref.shape
    cw = w_ref.shape[0]
    width = res_ref.shape[1]
    kvw = kw_ref.shape[1]
    nquery = q_ref.shape[0]
    heads = kvw // HEAD_DIM
    group = Y * cw

    img = lax.axis_index("img")
    tp = lax.axis_index("tp")
    zh = lax.div(img, X * Y)
    x = lax.rem(lax.div(img, Y), X)
    y = lax.rem(img, Y)
    zl = lax.div(tp, CORES)
    c = lax.rem(tp, CORES)

    def dev(dzh=0, dx=0, dy=0, dzl=0, dc=0):
        a = lax.rem(zh + dzh, ZH)
        b = lax.rem(x + dx + X, X)
        d = lax.rem(y + dy + Y, Y)
        e = lax.rem(zl + dzl + ZL, ZL)
        f = lax.rem(c + dc, CORES)
        return ((a * X + b) * Y + d, e * CORES + f)

    used = [0]
    pending = []

    def arranged(dst, src):
        for p, r in enumerate(ARRIVAL):
            dst[p * cw : (p + 1) * cw, :] = src[r * cw : (r + 1) * cw, :]

    def copy(src, dst, device):
        n = used[0]
        used[0] += 1
        assert n < COPIES
        return pltpu.make_async_remote_copy(
            src_ref=src,
            dst_ref=dst,
            send_sem=ss.at[n],
            recv_sem=rs.at[n],
            device_id=device,
            device_id_type=MESH,
        )

    def send(src, dst, device):
        cp = copy(src, dst, device)
        cp.start()
        pending.append(cp)
        return cp

    partners = (
        [dev(dzh=1)]
        + [dev(dy=d) for d in range(1, Y)]
        + [dev(dx=d) for d in range(1, X)]
        + [dev(dzl=d) for d in range(1, ZL)]
        + [dev(dc=1)]
        + [dev(dx=d, dzl=-d, dc=k) for d in range(1, X) for k in range(CORES)]
    )
    barrier = pltpu.get_barrier_semaphore()
    for partner in partners:
        pl.semaphore_signal(barrier, inc=1, device_id=partner, device_id_type=MESH)

    owner_x = lax.rem(x - zl + X, X)
    start, shift = window((lax.rem(zh + c, ZH) * X + owner_x) * group, 128)
    loads = [
        pltpu.make_async_copy(src, dst, ls.at[n])
        for n, (src, dst) in enumerate(
            (
                (w_ref, w_v),
                (kw_ref, kvl.at[0, 0, :, pl.ds(0, kvw)]),
                (vw_ref, kvl.at[0, 0, :, pl.ds(kvw, kvw)]),
                (hidden_ref, hidden_v),
                (gain_ref, gain_v),
                (res_ref.at[:, pl.ds(start, 512)], res_v),
                (q_ref, q_v),
            )
        )
    ]
    for cp in loads:
        cp.start()

    loads[0].wait()
    own32[0:cw, :] = w_v[...].astype(F32)
    own32[cw : cw + 1, :] = jnp.full((1, depth), dest_ref[0].astype(F32), F32)
    own32[cw + 1 : cw + 2, :] = jnp.full((1, depth), off_ref[0].astype(F32), F32)
    wl = (wl_a, wl_b)
    cut = wl_a.shape[-1]
    wl_a[0, 0] = own32[:, 0:cut].astype(BF16)
    wl_b[0, 0] = own32[:, cut:depth].astype(BF16)
    pl.semaphore_wait(barrier, len(partners))

    w_zh = [send(w.at[0, 0], w.at[1, 0], dev(dzh=1)) for w in wl]
    right, left = {}, {}

    def begin(h, a):
        right[h, a, 1] = send(wl[a].at[h, 0], wl[a].at[h, Y - 1], dev(dy=1))
        left[h, a, 1] = send(wl[a].at[h, 0], wl[a].at[h, 1], dev(dy=-1))

    for a in range(2):
        begin(0, a)
    loads[1].wait()
    loads[2].wait()
    kv_zh = send(kvl.at[0, 0], kvl.at[1, 0], dev(dzh=1))
    loads[3].wait()
    act[0] = jax.nn.gelu(hidden_v[...].astype(F32)).astype(BF16)
    act_x = [send(act.at[0], act.at[X - d], dev(dx=d)) for d in FAR_X]

    loads[5].wait()
    res_t[...] = res_v[...].astype(F32).T.astype(BF16)
    shift = pl.multiple_of(shift, 16)
    res_cp = copy(res_t.at[pl.ds(shift, group)], res_in, dev(dx=-zl))

    @pl.when(zl != 0)
    def _():
        res_cp.start()

    @pl.when(zl == 0)
    def _():
        res_in[...] = res_t[pl.ds(shift, group), :]

    for a in range(2):
        w_zh[a].wait_recv()
        begin(1, a)

    turn = lax.rem(group - cw * y, group)
    start_g, shift_g = window((lax.rem(zh + c, ZH) * X + x) * group, 128)
    loads[4].wait()
    for k in range(4):
        line = gain_v[pl.ds(lax.div(start_g, 128) + k, 1), :]
        gain_t[k * 128 : (k + 1) * 128, :] = jnp.broadcast_to(line, (128, 128)).T
    turned[...] = pltpu.roll(gain_t[pl.ds(pl.multiple_of(shift_g, 16), group), :], turn, 0)
    arranged(gain_t, turned)

    def pack(h, r):
        p = ARRIVAL.index(r)
        block = wl_a[h, r].astype(F32)
        w32[h, p * cw : p * cw + cw, 0:cut] = block[0:cw, :]
        top = cw // 8 * 8
        meta[h * Y + r, 0 : cw + 2 - top, :] = block[top : cw + 2, 0:kvw]
        w32[h, p * cw : p * cw + cw, cut:depth] = wl_b[h, r].astype(F32)[0:cw, :]

    def project(lo, hi):
        acts = jnp.concatenate([act[k] for k in range(X)], axis=1)
        for h in range(ZH):
            p = jnp.dot(w32[h, lo:hi].astype(BF16), acts, preferred_element_type=F32)
            part_f[h, lo:hi] = p
            part_b[h, lo:hi] = p.astype(BF16)
        return send(part_b.at[1 - c, pl.ds(lo, hi - lo)], part_x.at[pl.ds(lo, hi - lo)], dev(dc=1))

    def scatter(lo, hi, core_cp):
        core_cp.wait_recv()
        both = part_f[c, lo:hi] + part_x[lo:hi].astype(F32)
        for k in range(X):
            blk = both[:, k * patches : (k + 1) * patches]
            half_f[k, lo:hi] = blk
            half_b[k, lo:hi] = blk.astype(BF16)
        return [
            send(
                half_b.at[lax.rem(zl + d, ZL), pl.ds(lo, hi - lo)],
                half_r.at[d - 1, pl.ds(lo, hi - lo)],
                dev(dzl=d),
            )
            for d in range(1, ZL)
        ]

    early = 5 * cw // 16 * 16

    def ring(s):
        for h in range(ZH):
            for a in range(2):
                w = wl[a]
                right[h, a, s].wait_recv()
                if s < Y // 2 - 1 or (s < Y // 2 and h == 0):
                    right[h, a, s + 1] = send(w.at[h, Y - s], w.at[h, Y - s - 1], dev(dy=1))
                left[h, a, s].wait_recv()
                if s < Y // 2 - 1 or (s < Y // 2 and h == 1):
                    left[h, a, s + 1] = send(w.at[h, s], w.at[h, s + 1], dev(dy=-1))

    pack(0, 0)
    pack(1, 0)
    ring(1)
    for h in range(ZH):
        pack(h, 1)
        pack(h, Y - 1)
    ring(2)
    for h in range(ZH):
        pack(h, 2)
        pack(h, Y - 2)
    for cp in act_x:
        cp.wait_recv()
    early_cp = project(0, early)
    ring(3)
    early_sums = scatter(0, early, early_cp)
    for h in range(ZH):
        pack(h, 3)
        pack(h, Y - 3)
    for a in range(2):
        right[0, a, Y // 2].wait_recv()
    pack(0, Y // 2)
    for a in range(2):
        left[1, a, Y // 2].wait_recv()
    pack(1, Y // 2)
    late_cp = project(early, group)

    kv_zh.wait_recv()
    kv_y = [send(kvl.at[h, 0], kvl.at[h, Y - d], dev(dy=d)) for h in range(ZH) for d in FAR_Y]

    late_sums = scatter(early, group, late_cp)

    @pl.when(zl != 0)
    def _():
        res_cp.wait_recv()

    turned[...] = pltpu.roll(res_in[...].astype(F32), turn, 0)
    arranged(resid, turned)
    total = half_f[zl] + resid[...]
    for cp in early_sums + late_sums:
        cp.wait_recv()
    for d in range(1, ZL):
        total = total + half_r[d - 1].astype(F32)

    tall = total.reshape(group // 8, 8, patches)
    stats[0, 0:8] = jnp.sum(tall, axis=0)
    stats[0, 8:16] = jnp.sum(tall * tall, axis=0)
    st = []
    for d in range(X):
        for k in range(CORES):
            if d or k:
                st.append(send(stats.at[0], stats.at[d * CORES + k], dev(dx=d, dzl=-d, dc=k)))
    for cp in st:
        cp.wait_recv()
    both = jnp.sum(stats[...], axis=0)
    mean = jnp.sum(both[0:8], axis=0, keepdims=True) / width
    var = jnp.sum(both[8:16], axis=0, keepdims=True) / width - mean * mean
    normed[c, zl] = ((total - mean) * lax.rsqrt(var + EPS) * gain_t[0:group, :]).astype(BF16)

    ag = [send(normed.at[c, zl], normed.at[c, zl], dev(dzl=d)) for d in range(1, ZL)]
    fw = [send(normed.at[c, zl], normed.at[c, zl], dev(dc=1))]

    for cp in kv_y:
        cp.wait_recv()
    for h in range(ZH):
        for r in range(Y):
            p = ARRIVAL.index(r)
            kv32[h, p * cw : p * cw + cw, :] = kvl[h, r].astype(F32)

    for d in range(1, ZL):
        ag[d - 1].wait_recv()
        slot = normed.at[c, lax.rem(zl - d + ZL, ZL)]
        fw.append(send(slot, slot, dev(dc=1)))
    for cp in fw:
        cp.wait_recv()

    acc = None
    for h in range(ZH):
        nt = jnp.concatenate([normed[h, k] for k in range(X)], axis=1)
        p = lax.dot_general(
            kv32[h].astype(BF16), nt, (((0,), (0,)), ((), ())), preferred_element_type=F32
        )
        acc = p if acc is None else acc + p
    for d in range(1, X):
        kv_s[d - 1] = acc[:, d * patches : (d + 1) * patches].astype(BF16)
    kvs = [send(kv_s.at[d - 1], kv_r.at[d - 1], dev(dx=d)) for d in FAR_X]
    kv = acc[:, 0:patches]
    for cp in kvs:
        cp.wait_recv()
    for d in range(1, X):
        kv = kv + kv_r[d - 1].astype(F32)
    kv = kv.astype(BF16)

    loads[6].wait()

    def attend(n):
        kt = kv[n * HEAD_DIM : (n + 1) * HEAD_DIM, :]
        vt = kv[kvw + n * HEAD_DIM : kvw + (n + 1) * HEAD_DIM, :]
        q = q_v[:, n * HEAD_DIM : (n + 1) * HEAD_DIM]
        scores = jnp.dot(q, kt, preferred_element_type=F32) * (1.0 / HEAD_DIM**0.5)
        expo = jnp.exp(scores - jnp.max(scores, axis=1, keepdims=True))
        weights = (expo / jnp.sum(expo, axis=1, keepdims=True)).astype(BF16)
        mixed = lax.dot_general(
            weights, vt, (((1,), (1,)), ((), ())), preferred_element_type=F32
        )
        rows[n, 0, 0] = mixed.astype(BF16)
        return send(rows.at[n, 0, 0], rows.at[n, 1, 0], dev(dzh=1))

    def spread(n, h):
        return {
            d: send(rows.at[n, h, 0], rows.at[n, h, Y - d], dev(dy=d)) for d in (2, Y - 2, 1, Y - 1)
        }

    def relay(n, h, first):
        out = []
        for sign, d in ((1, 2), (-1, Y - 2)):
            first[d].wait_recv()
            slot = (Y - 2 * sign) % Y
            block = rows.at[n, h, slot]
            if sign == (1 if h == 0 else -1):
                out.append(send(block, rows.at[n, h, Y // 2], dev(dy=2 * sign)))
            out.append(send(block, rows.at[n, h, slot - sign], dev(dy=sign)))
        return out + [first[1], first[Y - 1]]

    skip = cw - cw // 8 * 8

    def pick(n):
        for k in range(X):
            shard = ((zh * X + lax.rem(x + k, X)) * Y + y).astype(F32)
            for s in range(MOST_IMG):
                picked = None
                for m in range(ZH * Y):
                    here = (meta[m, skip : skip + 1, 0:HEAD_DIM] == shard) & (
                        meta[m, skip + 1 : skip + 2, 0:HEAD_DIM] == float(s * nquery)
                    )
                    term = rows[n, m // Y, m % Y] * jnp.where(here, 1.0, 0.0).astype(BF16)
                    picked = term if picked is None else picked + term
                slab[n, k, s * nquery : (s + 1) * nquery, :] = picked
        return [send(slab.at[n, d], slab_r.at[n, d - 1], dev(dx=d)) for d in FAR_X]

    r_zh, got, slabs = [], [[] for _ in range(heads)], []
    first = {}
    r_zh.append(attend(0))
    first[0, 0] = spread(0, 0)
    for n in range(1, heads):
        r_zh.append(attend(n))
    for n in range(heads):
        r_zh[n].wait_recv()
        first[n, 1] = spread(n, 1)
        if n + 1 < heads:
            first[n + 1, 0] = spread(n + 1, 0)
        for h in range(ZH):
            got[n] += relay(n, h, first[n, h])
    for n in range(heads):
        for cp in got[n]:
            cp.wait_recv()
        slabs.append(pick(n))
    for n in range(heads):
        for cp in slabs[n]:
            cp.wait_recv()
        result = slab[n, 0]
        for d in range(1, X):
            result = result + slab_r[n, d - 1]
        out_ref[:, n * HEAD_DIM : (n + 1) * HEAD_DIM] = result

    @pl.when(zl != 0)
    def _():
        res_cp.wait_send()

    for cp in pending:
        cp.wait_send()


def local(
    vit_hidden,
    residual_stream,
    fc2_weight,
    ln_gain,
    key_weight,
    value_weight,
    query_heads,
    dest_shard,
    row_offset,
):
    patches, depth = vit_hidden.shape
    cw = fc2_weight.shape[1]
    kvw = key_weight.shape[1]
    nquery = query_heads.shape[0]
    width = residual_stream.shape[1]
    group = Y * cw
    shard_rows = MOST_IMG * nquery
    heads = kvw // HEAD_DIM
    cut = depth // 2 // 128 * 128 + 128
    vmem = pl.BlockSpec(memory_space=pltpu.VMEM)
    smem = pl.BlockSpec(memory_space=pltpu.SMEM)
    return pl.pallas_call(
        kernel,
        out_shape=jax.ShapeDtypeStruct((shard_rows, kvw), BF16),
        in_specs=[pl.BlockSpec(memory_space=pltpu.HBM)] * 7 + [smem] * 2,
        out_specs=vmem,
        scratch_shapes=[
            pltpu.VMEM((X, depth, patches), BF16),
            pltpu.VMEM((ZH, Y, cw + 2, cut), BF16),
            pltpu.VMEM((ZH, Y, cw + 2, depth - cut), BF16),
            pltpu.VMEM((ZH, Y, cw, 2 * kvw), BF16),
            pltpu.VMEM((cw + 2, depth), F32),
            pltpu.VMEM((ZH * Y, 8, kvw), F32),
            pltpu.VMEM((ZH, group, depth), F32),
            pltpu.VMEM((ZH, group, 2 * kvw), F32),
            pltpu.VMEM((512, 128), BF16),
            pltpu.VMEM((group, patches), BF16),
            pltpu.VMEM((group, patches), F32),
            pltpu.VMEM((group, patches), F32),
            pltpu.VMEM((512, 128), F32),
            pltpu.VMEM((ZH, group, X * patches), F32),
            pltpu.VMEM((ZH, group, X * patches), BF16),
            pltpu.VMEM((group, X * patches), BF16),
            pltpu.VMEM((X, group, patches), F32),
            pltpu.VMEM((X, group, patches), BF16),
            pltpu.VMEM((ZL - 1, group, patches), BF16),
            pltpu.VMEM((X * CORES, 16, patches), F32),
            pltpu.VMEM((ZH, X, group, patches), BF16),
            pltpu.VMEM((X - 1, 2 * kvw, patches), BF16),
            pltpu.VMEM((X - 1, 2 * kvw, patches), BF16),
            pltpu.VMEM((heads, ZH, Y, nquery, HEAD_DIM), BF16),
            pltpu.VMEM((heads, X, shard_rows, HEAD_DIM), BF16),
            pltpu.VMEM((heads, X - 1, shard_rows, HEAD_DIM), BF16),
            pltpu.SemaphoreType.DMA((COPIES,)),
            pltpu.SemaphoreType.DMA((COPIES,)),
            pltpu.SemaphoreType.DMA((7,)),
            pltpu.VMEM((depth, patches), BF16),
            pltpu.VMEM((patches, 512), BF16),
            pltpu.VMEM((cw, depth), BF16),
            pltpu.VMEM((width // 128, 128), F32),
            pltpu.VMEM((nquery, kvw), BF16),
        ],
        compiler_params=pltpu.CompilerParams(
            collective_id=0, has_side_effects=True, vmem_limit_bytes=63 * 2**20
        ),
        cost_estimate=pl.CostEstimate(
            flops=1100000000, bytes_accessed=3000000, transcendentals=200000
        ),
        name="encoder_resampler",
    )(
        vit_hidden.T,
        residual_stream,
        fc2_weight.T,
        ln_gain.reshape(width // 128, 128),
        key_weight,
        value_weight,
        query_heads,
        dest_shard,
        row_offset,
    )


def solution(mesh):
    return jax.shard_map(
        local,
        mesh=mesh,
        in_specs=(
            P("img", "tp"),
            P("img", None),
            P("tp", "img"),
            P(),
            P("img", "tp"),
            P("img", "tp"),
            P(None, "tp"),
            P("img"),
            P("img"),
        ),
        out_specs=P("img", "tp"),
        check_vma=False,
    )
```

```python
import functools

import jax
import jax.numpy as jnp
from jax import lax
from jax.experimental import pallas as pl
from jax.experimental.pallas import tpu as pltpu
from jax.sharding import PartitionSpec as P

HEAD_DIM = 128
MOST_IMG = 4
ZH, X, Y, ZL, CORES = 2, 4, 8, 4, 2
EPS = 1e-06
MESH = pl.DeviceIdType.MESH
F32 = jnp.float32
BF16 = jnp.bfloat16
COPIES = 160
ARRIVAL = (0, 1, 7, 2, 6, 3, 5, 4)
FAR_X = (2, 1, 3)


def window(base, align):
    start = lax.div(base, align) * align
    return pl.multiple_of(start, align), base - start


def kernel(
    hidden_ref,
    res_ref,
    w_ref,
    gain_ref,
    kw_ref,
    vw_ref,
    q_ref,
    dest_ref,
    off_ref,
    out_ref,
    act,
    wl_a,
    wl_b,
    kvl,
    own32,
    meta,
    w32,
    kv32,
    kvt_e,
    kvt_l,
    tilt,
    u_all,
    fin,
    kv_acc,
    res_t,
    res_in,
    turned,
    resid,
    gain_t,
    gain_c,
    part_f,
    part_b,
    part_x,
    half_f,
    half_b,
    half_r,
    stats_e,
    stats_l,
    scale,
    normed,
    kv_own,
    kv_s,
    kv_r,
    rows,
    slab,
    slab_r,
    ss,
    rs,
    ls,
    hidden_v,
    res_v,
    w_v,
    gain_v,
    q_v,
    kw_v,
    vw_v,
    dest_s,
    off_s,
):
    depth, patches = hidden_ref.shape
    cw = w_ref.shape[0]
    width = res_ref.shape[1]
    kvw = kw_ref.shape[1]
    nquery = q_ref.shape[0]
    heads = kvw // HEAD_DIM
    group = Y * cw

    img = lax.axis_index("img")
    tp = lax.axis_index("tp")
    zh = lax.div(img, X * Y)
    x = lax.rem(lax.div(img, Y), X)
    y = lax.rem(img, Y)
    zl = lax.div(tp, CORES)
    c = lax.rem(tp, CORES)

    def dev(dzh=0, dx=0, dy=0, dzl=0, dc=0):
        a = lax.rem(zh + dzh, ZH)
        b = lax.rem(x + dx + X, X)
        d = lax.rem(y + dy + Y, Y)
        e = lax.rem(zl + dzl + ZL, ZL)
        f = lax.rem(c + dc, CORES)
        return ((a * X + b) * Y + d, e * CORES + f)

    used = [0]
    pending = []

    def arranged(dst, src):
        for p, r in enumerate(ARRIVAL):
            dst[p * cw : (p + 1) * cw, :] = src[r * cw : (r + 1) * cw, :]

    def copy(src, dst, device):
        n = used[0]
        used[0] += 1
        assert n < COPIES
        return pltpu.make_async_remote_copy(
            src_ref=src,
            dst_ref=dst,
            send_sem=ss.at[n],
            recv_sem=rs.at[n],
            device_id=device,
            device_id_type=MESH,
        )

    def send(src, dst, device):
        cp = copy(src, dst, device)
        cp.start()
        pending.append(cp)
        return cp

    def spread(ref, h):
        return {d: send(ref.at[h, 0], ref.at[h, Y - d], dev(dy=d)) for d in (2, Y - 2, 1, Y - 1)}

    def relay(ref, h, first):
        out = []
        for sign, d in ((1, 2), (-1, Y - 2)):
            first[d].wait_recv()
            slot = (Y - 2 * sign) % Y
            block = ref.at[h, slot]
            if sign == (1 if h == 0 else -1):
                out.append(send(block, ref.at[h, Y // 2], dev(dy=2 * sign)))
            out.append(send(block, ref.at[h, slot - sign], dev(dy=sign)))
        return out + [first[1], first[Y - 1]]

    partners = (
        [dev(dzh=1)]
        + [dev(dy=d) for d in range(1, Y)]
        + [dev(dx=d) for d in range(1, X)]
        + [dev(dzl=d) for d in range(1, ZL)]
        + [dev(dc=1)]
        + [dev(dx=d, dzl=-d, dc=k) for d in range(1, X) for k in range(CORES)]
        + [dev(dzl=d, dc=1) for d in range(1, ZL)]
    )
    barrier = pltpu.get_barrier_semaphore()
    for partner in partners:
        pl.semaphore_signal(barrier, inc=1, device_id=partner, device_id_type=MESH)

    owner_x = lax.rem(x - zl + X, X)
    start, shift = window((lax.rem(zh + c, ZH) * X + owner_x) * group, 128)
    loads = [
        pltpu.make_async_copy(src, dst, ls.at[n])
        for n, (src, dst) in enumerate(
            (
                (w_ref, w_v),
                (kw_ref, kw_v),
                (vw_ref, vw_v),
                (hidden_ref, hidden_v),
                (gain_ref, gain_v),
                (res_ref.at[:, pl.ds(start, 512)], res_v),
                (q_ref, q_v),
                (dest_ref, dest_s),
                (off_ref, off_s),
            )
        )
    ]
    for cp in loads:
        cp.start()

    tall_rows = own32.shape[0]
    own32[...] = jnp.zeros(own32.shape, F32)
    kvl[0, 0] = jnp.zeros((tall_rows, 2 * kvw), BF16)
    loads[0].wait()
    loads[7].wait()
    loads[8].wait()
    own32[0:cw, 0:depth] = w_v[...].astype(F32)
    own32[cw : cw + 1, 0:depth] = jnp.full((1, depth), dest_s[0].astype(F32), F32)
    own32[cw + 1 : cw + 2, 0:depth] = jnp.full((1, depth), off_s[0].astype(F32), F32)
    wl = (wl_a, wl_b)
    cut = wl_a.shape[-1]
    wl_a[0, 0] = own32[:, 0:cut].astype(BF16)
    wl_b[0, 0] = own32[:, cut:].astype(BF16)
    pl.semaphore_wait(barrier, len(partners))

    w_zh = [send(wl_a.at[0, 0], wl_a.at[1, 0], dev(dzh=1))]
    right, left = {}, {}

    def begin(h, a):
        right[h, a, 1] = send(wl[a].at[h, 0], wl[a].at[h, Y - 1], dev(dy=1))
        left[h, a, 1] = send(wl[a].at[h, 0], wl[a].at[h, 1], dev(dy=-1))

    def sent(*cps):
        for cp in cps:
            cp.wait_send()
            pending[:] = [p for p in pending if p is not cp]

    begin(0, 0)
    loads[1].wait()
    loads[2].wait()
    kvl[0, 0, 0:cw, 0:kvw] = kw_v[...]
    kvl[0, 0, 0:cw, kvw : 2 * kvw] = vw_v[...]
    sent(right[0, 0, 1], left[0, 0, 1])
    begin(0, 1)
    sent(w_zh[0])
    w_zh.append(send(wl_b.at[0, 0], wl_b.at[1, 0], dev(dzh=1)))
    loads[3].wait()
    act[0] = jax.nn.gelu(hidden_v[...].astype(F32)).astype(BF16)
    act_x = [send(act.at[0], act.at[X - d], dev(dx=d)) for d in FAR_X]

    loads[5].wait()
    res_t[...] = res_v[...].astype(F32).T.astype(BF16)
    shift = pl.multiple_of(shift, 16)
    res_cp = copy(res_t.at[pl.ds(shift, group)], res_in, dev(dx=-zl))

    @pl.when(zl != 0)
    def _():
        res_cp.start()

    @pl.when(zl == 0)
    def _():
        res_in[...] = res_t[pl.ds(shift, group), :]

    turn = lax.rem(group - cw * y, group)

    def columns():
        loads[4].wait()
        for h in range(ZH):
            start_g, shift_g = window((lax.rem(zh + h, ZH) * X + x) * group, 128)
            for k in range(4):
                line = gain_v[pl.ds(lax.div(start_g, 128) + k, 1), :]
                gain_t[k * 128 : (k + 1) * 128, :] = jnp.broadcast_to(line, (128, 128)).T
            turned[...] = pltpu.roll(gain_t[pl.ds(pl.multiple_of(shift_g, 16), group), :], turn, 0)
            arranged(gain_c.at[h], turned)

    def pack(h, r):
        p = ARRIVAL.index(r)
        block = wl_a[h, r].astype(F32)
        w32[h, p * cw : p * cw + cw, 0:cut] = block[0:cw, :]
        top = cw // 8 * 8
        meta[h * Y + r] = block[top : top + 8, 0:kvw]
        w32[h, p * cw : p * cw + cw, cut:depth] = wl_b[h, r].astype(F32)[0:cw, 0 : depth - cut]

    def project(lo, hi):
        acts = jnp.concatenate([act[k] for k in range(X)], axis=1)
        for h in range(ZH):
            p = jnp.dot(w32[h, lo:hi].astype(BF16), acts, preferred_element_type=F32)
            part_f[h, lo:hi] = p
            part_b[h, lo:hi] = p.astype(BF16)
        return send(part_b.at[1 - c, pl.ds(lo, hi - lo)], part_x.at[pl.ds(lo, hi - lo)], dev(dc=1))

    def scatter(lo, hi, core_cp):
        core_cp.wait_recv()
        both = part_f[c, lo:hi] + part_x[lo:hi].astype(F32)
        for k in range(X):
            blk = both[:, k * patches : (k + 1) * patches]
            half_f[k, lo:hi] = blk
            half_b[k, lo:hi] = blk.astype(BF16)
        return [
            send(
                half_b.at[lax.rem(zl + d, ZL), pl.ds(lo, hi - lo)],
                half_r.at[d - 1, pl.ds(lo, hi - lo)],
                dev(dzl=d),
            )
            for d in range(1, ZL)
        ]

    early = kvt_e.shape[-1]

    def ring(h, a, s):
        w = wl[a]
        if s < Y // 2 or h == 0:
            right[h, a, s].wait_recv()
        if s < Y // 2 - 1 or (s < Y // 2 and h == 0):
            right[h, a, s + 1] = send(w.at[h, Y - s], w.at[h, Y - s - 1], dev(dy=1))
        if s < Y // 2 or h == 1:
            left[h, a, s].wait_recv()
        if s < Y // 2 - 1 or (s < Y // 2 and h == 1):
            left[h, a, s + 1] = send(w.at[h, s], w.at[h, s + 1], dev(dy=-1))

    def finish(lo, hi, sums, pivot):
        total = half_f[zl, lo:hi] + resid[lo:hi]
        for cp in sums:
            cp.wait_recv()
        for d in range(1, ZL):
            total = total + half_r[d - 1, lo:hi].astype(F32)
        tall = total.reshape((hi - lo) // 8, 8, patches)
        once, twice = jnp.sum(tall, axis=0), jnp.sum(tall * tall, axis=0)
        if pivot is None:
            pivot = jnp.sum(once, axis=0, keepdims=True) / (hi - lo)
        normed[c, zl, lo:hi] = ((total - pivot) * gain_c[c, lo:hi]).astype(BF16)

        def block(k):
            return normed.at[c, k, pl.ds(lo, hi - lo)]

        ag = [send(block(zl), block(zl), dev(dzl=d)) for d in range(1, ZL)]
        fw = [send(block(zl), block(zl), dev(dc=1))]

        def forward(d):
            ag[d - 1].wait_recv()
            k = lax.rem(zl - d + ZL, ZL)
            fw.append(send(block(k), block(k), dev(dc=1)))

        return once, twice, pivot, fw, forward

    def exchange(ref):
        return [
            send(ref.at[0], ref.at[d * CORES + k], dev(dx=d, dzl=-d, dc=k))
            for d in range(X)
            for k in range(CORES)
            if d or k
        ]

    ring(0, 0, 1)
    ring(0, 1, 1)
    ring(0, 0, 2)
    w_zh[0].wait_recv()
    begin(1, 0)
    ring(0, 1, 2)
    w_zh[1].wait_recv()
    begin(1, 1)
    kv_zh = send(kvl.at[0, 0], kvl.at[1, 0], dev(dzh=1))
    columns()
    pack(1, 0)
    for r in (0, 1, Y - 1):
        pack(0, r)
    ring(0, 0, 3)
    ring(1, 0, 1)
    ring(0, 1, 3)
    ring(1, 1, 1)
    for r in (1, Y - 1):
        pack(1, r)
    for cp in act_x:
        cp.wait_recv()
    early_cp = project(0, early)
    ring(0, 0, 4)
    ring(1, 0, 2)
    ring(0, 1, 4)
    ring(1, 1, 2)
    early_sums = scatter(0, early, early_cp)
    for r in (2, Y - 2, 3, Y - 3, 4):
        pack(0, r)
    for r in (2, Y - 2):
        pack(1, r)

    @pl.when(zl != 0)
    def _():
        res_cp.wait_recv()

    turned[...] = pltpu.roll(res_in[...].astype(F32), turn, 0)
    arranged(resid, turned)
    ring(1, 0, 3)
    ring(1, 1, 3)
    once_e, twice_e, here_e, fw_e, forward_e = finish(0, early, early_sums, None)
    stats_e[0] = once_e
    st_e = exchange(stats_e)
    for r in (3, Y - 3):
        pack(1, r)
    ring(1, 0, 4)
    ring(1, 1, 4)
    pack(1, 4)
    late_cp = project(early, group)

    kv_zh.wait_recv()
    kv_first = [spread(kvl, h) for h in range(ZH)]

    late_sums = scatter(early, group, late_cp)
    kv_y = [cp for h in range(ZH) for cp in relay(kvl, h, kv_first[h])]

    for cp in st_e:
        cp.wait_recv()
    sum_e = jnp.sum(jnp.sum(stats_e[...], axis=0), axis=0, keepdims=True)
    pivot = sum_e / (X * CORES * early)
    once_l, twice_l, _, fw_l, forward_l = finish(early, group, late_sums, pivot)
    stats_l[0, 0:8] = once_l
    stats_l[0, 8:16] = twice_e + twice_l
    st_l = exchange(stats_l)
    scale[c, zl] = jnp.broadcast_to(here_e - pivot, (8, patches))
    sc = [
        send(scale.at[c, zl], scale.at[c, zl], dev(dzl=d, dc=k))
        for d in range(ZL)
        for k in range(CORES)
        if d or k
    ]
    for d in range(1, ZL):
        forward_e(d)

    for cp in kv_y:
        cp.wait_recv()
    for h in range(ZH):
        for r in range(Y):
            p = ARRIVAL.index(r)
            kv32[p * cw : p * cw + cw, :] = kvl[h, r].astype(F32)[0:cw, :]
        kvt_e[h] = kv32[0:early].T.astype(BF16)
        kvt_l[h] = kv32[early:group].T.astype(BF16)
        tilt[h] = jnp.dot(
            kvt_e[h], gain_c[h, 0:early].astype(BF16), preferred_element_type=F32
        )
        u = lax.dot_general(
            gain_c[h].astype(BF16),
            kv32[...].astype(BF16),
            (((0,), (0,)), ((), ())),
            preferred_element_type=F32,
        )[0:8]
        weighted = u if h == 0 else weighted + u
    u_all[0] = weighted
    us = [send(u_all.at[0], u_all.at[X - d], dev(dx=d)) for d in FAR_X]

    for cp in fw_e + sc:
        cp.wait_recv()
    acc = None
    for h in range(ZH):
        nt = jnp.concatenate([normed[h, k, 0:early] for k in range(X)], axis=1)
        p = jnp.dot(kvt_e[h], nt, preferred_element_type=F32)
        acc = p if acc is None else acc + p
    for k in range(X):
        part = acc[:, k * patches : (k + 1) * patches]
        for h in range(ZH):
            part = part + tilt[h] * scale[h, k, 0:1, :]
        kv_acc[k] = part
    base = used[0]
    used[0] += X

    def kv_copy(k):
        return pltpu.make_async_remote_copy(
            src_ref=kv_s.at[k],
            dst_ref=kv_r.at[k],
            send_sem=ss.at[base + k],
            recv_sem=rs.at[base + k],
            device_id=dev(dx=k),
            device_id_type=MESH,
        )

    for d in range(ZL):
        k = lax.rem(zl - d + ZL, ZL)
        if d == 1:
            for e in range(1, ZL):
                forward_l(e)
        fw_l[d].wait_recv()
        part = kv_acc[k]
        for h in range(ZH):
            part = part + jnp.dot(
                kvt_l[h], normed[h, k, early:group], preferred_element_type=F32
            )

        @pl.when(k == 0)
        def _():
            kv_own[...] = part

        @pl.when(k != 0)
        def _():
            kv_s[k] = part.astype(BF16)
            kv_copy(k).start()

    for cp in st_l:
        cp.wait_recv()
    fin_cps = [copy(fin, fin, dev(dzl=d)) for d in range(1, ZL)]

    @pl.when(zl == 0)
    def _():
        both = jnp.sum(stats_l[...], axis=0)
        mean = (sum_e + jnp.sum(both[0:8], axis=0, keepdims=True)) / width
        var = jnp.sum(both[8:16], axis=0, keepdims=True) / width - mean * mean
        fin[0:8] = jnp.broadcast_to(lax.rsqrt(var + EPS), (8, patches))
        first_row = lax.broadcasted_iota(jnp.int32, (8, patches), 0) == 0
        fin[8:16] = jnp.where(first_row, jnp.broadcast_to(pivot - mean, (8, patches)), 0.0)
        for cp in fin_cps:
            cp.start()

    for d in range(1, ZL):

        @pl.when(zl == d)
        def _():
            fin_cps[d - 1].wait_recv()

    for cp in us:
        cp.wait_recv()
    kv = kv_own[...] + lax.dot_general(
        jnp.sum(u_all[...], axis=0),
        fin[8:16],
        (((0,), (0,)), ((), ())),
        precision=lax.Precision.HIGHEST,
        preferred_element_type=F32,
    )
    for k in range(1, X):
        kv_copy(k).wait_recv()
    for k in range(1, X):
        kv = kv + kv_r[k].astype(F32)
    kv = (kv * fin[0:1, :]).astype(BF16)

    loads[6].wait()

    def attend(n):
        kt = kv[n * HEAD_DIM : (n + 1) * HEAD_DIM, :]
        vt = kv[kvw + n * HEAD_DIM : kvw + (n + 1) * HEAD_DIM, :]
        q = q_v[:, n * HEAD_DIM : (n + 1) * HEAD_DIM]
        scores = jnp.dot(q, kt, preferred_element_type=F32) * (1.0 / HEAD_DIM**0.5)
        expo = jnp.exp(scores - jnp.max(scores, axis=1, keepdims=True))
        weights = (expo / jnp.sum(expo, axis=1, keepdims=True)).astype(BF16)
        mixed = lax.dot_general(
            weights, vt, (((1,), (1,)), ((), ())), preferred_element_type=F32
        )
        rows[n, 0, 0] = mixed.astype(BF16)
        return send(rows.at[n, 0, 0], rows.at[n, 1, 0], dev(dzh=1))

    skip = cw - cw // 8 * 8

    def pick(n):
        for k in range(X):
            shard = ((zh * X + lax.rem(x + k, X)) * Y + y).astype(F32)
            for s in range(MOST_IMG):
                picked = None
                for m in range(ZH * Y):
                    here = (meta[m, skip : skip + 1, 0:HEAD_DIM] == shard) & (
                        meta[m, skip + 1 : skip + 2, 0:HEAD_DIM] == float(s * nquery)
                    )
                    term = rows[n, m // Y, m % Y] * jnp.where(here, 1.0, 0.0).astype(BF16)
                    picked = term if picked is None else picked + term
                slab[n, k, s * nquery : (s + 1) * nquery, :] = picked
        return [send(slab.at[n, d], slab_r.at[n, d - 1], dev(dx=d)) for d in FAR_X]

    r_zh, got, slabs = [], [[] for _ in range(heads)], []
    first = {}
    r_zh.append(attend(0))
    first[0, 0] = spread(rows.at[0], 0)
    for n in range(1, heads):
        r_zh.append(attend(n))
        first[n, 0] = spread(rows.at[n], 0)
    got[0] += relay(rows.at[0], 0, first[0, 0])
    for n in range(heads):
        r_zh[n].wait_recv()
        first[n, 1] = spread(rows.at[n], 1)
    for n in range(1, heads):
        got[n] += relay(rows.at[n], 0, first[n, 0])
    for n in range(heads):
        got[n] += relay(rows.at[n], 1, first[n, 1])
    for n in range(heads):
        for cp in got[n]:
            cp.wait_recv()
        slabs.append(pick(n))
    for n in range(heads):
        for cp in slabs[n]:
            cp.wait_recv()
        result = slab[n, 0]
        for d in range(1, X):
            result = result + slab_r[n, d - 1]
        out_ref[:, n * HEAD_DIM : (n + 1) * HEAD_DIM] = result

    @pl.when(zl != 0)
    def _():
        res_cp.wait_send()

    @pl.when(zl == 0)
    def _():
        for cp in fin_cps:
            cp.wait_send()

    for k in range(1, X):
        kv_copy(k).wait_send()
    for cp in pending:
        cp.wait_send()


def local(
    vit_hidden,
    residual_stream,
    fc2_weight,
    ln_gain,
    key_weight,
    value_weight,
    query_heads,
    dest_shard,
    row_offset,
):
    patches, depth = vit_hidden.shape
    cw = fc2_weight.shape[1]
    kvw = key_weight.shape[1]
    nquery = query_heads.shape[0]
    width = residual_stream.shape[1]
    group = Y * cw
    shard_rows = MOST_IMG * nquery
    heads = kvw // HEAD_DIM
    early = 3 * cw // 16 * 16
    tall = cw // 8 * 8 + 8
    wide = (depth + 127) // 128 * 128
    cut = depth // 2 // 128 * 128 + 128
    vmem = pl.BlockSpec(memory_space=pltpu.VMEM)
    return pl.pallas_call(
        kernel,
        out_shape=pltpu.VMEM((shard_rows, kvw), BF16),
        in_specs=[pl.BlockSpec(memory_space=pl.ANY)] * 9,
        out_specs=vmem,
        scratch_shapes=[
            pltpu.VMEM((X, depth, patches), BF16),
            pltpu.VMEM((ZH, Y, tall, cut), BF16),
            pltpu.VMEM((ZH, Y, tall, wide - cut), BF16),
            pltpu.VMEM((ZH, Y, tall, 2 * kvw), BF16),
            pltpu.VMEM((tall, wide), F32),
            pltpu.VMEM((ZH * Y, 8, kvw), F32),
            pltpu.VMEM((ZH, group, depth), F32),
            pltpu.VMEM((group, 2 * kvw), F32),
            pltpu.VMEM((ZH, 2 * kvw, early), BF16),
            pltpu.VMEM((ZH, 2 * kvw, group - early), BF16),
            pltpu.VMEM((ZH, 2 * kvw, patches), F32),
            pltpu.VMEM((X, 8, 2 * kvw), F32),
            pltpu.VMEM((16, patches), F32),
            pltpu.VMEM((X, 2 * kvw, patches), F32),
            pltpu.VMEM((512, 128), BF16),
            pltpu.VMEM((group, patches), BF16),
            pltpu.VMEM((group, patches), F32),
            pltpu.VMEM((group, patches), F32),
            pltpu.VMEM((512, 128), F32),
            pltpu.VMEM((ZH, group, 128), F32),
            pltpu.VMEM((ZH, group, X * patches), F32),
            pltpu.VMEM((ZH, group, X * patches), BF16),
            pltpu.VMEM((group, X * patches), BF16),
            pltpu.VMEM((X, group, patches), F32),
            pltpu.VMEM((X, group, patches), BF16),
            pltpu.VMEM((ZL - 1, group, patches), BF16),
            pltpu.VMEM((X * CORES, 8, patches), F32),
            pltpu.VMEM((X * CORES, 16, patches), F32),
            pltpu.VMEM((ZH, X, 8, patches), F32),
            pltpu.VMEM((ZH, X, group, patches), BF16),
            pltpu.VMEM((2 * kvw, patches), F32),
            pltpu.VMEM((X, 2 * kvw, patches), BF16),
            pltpu.VMEM((X, 2 * kvw, patches), BF16),
            pltpu.VMEM((heads, ZH, Y, nquery, HEAD_DIM), BF16),
            pltpu.VMEM((heads, X, shard_rows, HEAD_DIM), BF16),
            pltpu.VMEM((heads, X - 1, shard_rows, HEAD_DIM), BF16),
            pltpu.SemaphoreType.DMA((COPIES,)),
            pltpu.SemaphoreType.DMA((COPIES,)),
            pltpu.SemaphoreType.DMA((9,)),
            pltpu.VMEM((depth, patches), BF16),
            pltpu.VMEM((patches, 512), BF16),
            pltpu.VMEM((cw, depth), BF16),
            pltpu.VMEM((width // 128, 128), F32),
            pltpu.VMEM((nquery, kvw), BF16),
            pltpu.VMEM((cw, kvw), BF16),
            pltpu.VMEM((cw, kvw), BF16),
            pltpu.SMEM((1,), jnp.int32),
            pltpu.SMEM((1,), jnp.int32),
        ],
        compiler_params=pltpu.CompilerParams(
            collective_id=0, has_side_effects=True, vmem_limit_bytes=63 * 2**20
        ),
        cost_estimate=pl.CostEstimate(
            flops=1100000000, bytes_accessed=3000000, transcendentals=200000
        ),
        name="encoder_resampler",
    )(
        vit_hidden.T,
        residual_stream,
        fc2_weight.T,
        ln_gain.reshape(width // 128, 128),
        key_weight,
        value_weight,
        query_heads,
        dest_shard,
        row_offset,
    )


def solution(mesh):
    return jax.shard_map(
        local,
        mesh=mesh,
        in_specs=(
            P("img", "tp"),
            P("img", None),
            P("tp", "img"),
            P(),
            P("img", "tp"),
            P("img", "tp"),
            P(None, "tp"),
            P("img"),
            P("img"),
        ),
        out_specs=P("img", "tp"),
        check_vma=False,
    )
```

```python
import functools

import jax
import jax.numpy as jnp
from jax import lax
from jax.experimental import pallas as pl
from jax.experimental.pallas import tpu as pltpu
from jax.sharding import PartitionSpec as P

HEAD_DIM = 128
MOST_IMG = 4
ZH, X, Y, ZL, CORES = 2, 4, 8, 4, 2
EPS = 1e-06
MESH = pl.DeviceIdType.MESH
F32 = jnp.float32
BF16 = jnp.bfloat16
COPIES = 192
ARRIVAL = (0, 1, 7, 2, 6, 3, 5, 4)
FAR_X = (2, 1, 3)


def window(base, align):
    start = lax.div(base, align) * align
    return pl.multiple_of(start, align), base - start


def kernel(
    hidden_ref,
    res_ref,
    w_ref,
    gain_ref,
    kw_ref,
    vw_ref,
    q_ref,
    dest_ref,
    off_ref,
    out_ref,
    act,
    wl_a,
    wl_b,
    kvl,
    own32,
    meta,
    w32,
    kv32,
    kvt_e,
    kvt_l,
    tilt,
    u_all,
    fin,
    kv_acc,
    res_t,
    res_in,
    turned,
    resid,
    gain_t,
    gain_c,
    part_f,
    part_b,
    part_x,
    half_f,
    half_b,
    half_r,
    stats_e,
    stats_l,
    scale,
    normed,
    kv_own,
    kv_s,
    kv_r,
    rows,
    mask,
    slab,
    slab_r,
    ss,
    rs,
    ls,
    hidden_v,
    res_v,
    w_v,
    gain_v,
    q_v,
    kw_v,
    vw_v,
    dest_s,
    off_s,
):
    depth, patches = hidden_ref.shape
    cw = w_ref.shape[0]
    width = res_ref.shape[1]
    kvw = kw_ref.shape[1]
    nquery = q_ref.shape[0]
    heads = kvw // HEAD_DIM
    group = Y * cw

    img = lax.axis_index("img")
    tp = lax.axis_index("tp")
    zh = lax.div(img, X * Y)
    x = lax.rem(lax.div(img, Y), X)
    y = lax.rem(img, Y)
    zl = lax.div(tp, CORES)
    c = lax.rem(tp, CORES)

    def dev(dzh=0, dx=0, dy=0, dzl=0, dc=0):
        a = lax.rem(zh + dzh, ZH)
        b = lax.rem(x + dx + X, X)
        d = lax.rem(y + dy + Y, Y)
        e = lax.rem(zl + dzl + ZL, ZL)
        f = lax.rem(c + dc, CORES)
        return ((a * X + b) * Y + d, e * CORES + f)

    used = [0]
    pending = []

    def arranged(dst, src):
        for p, r in enumerate(ARRIVAL):
            dst[p * cw : (p + 1) * cw, :] = src[r * cw : (r + 1) * cw, :]

    def copy(src, dst, device):
        n = used[0]
        used[0] += 1
        assert n < COPIES
        return pltpu.make_async_remote_copy(
            src_ref=src,
            dst_ref=dst,
            send_sem=ss.at[n],
            recv_sem=rs.at[n],
            device_id=device,
            device_id_type=MESH,
        )

    def send(src, dst, device):
        cp = copy(src, dst, device)
        cp.start()
        pending.append(cp)
        return cp

    def spread(ref, h):
        return {d: send(ref.at[h, 0], ref.at[h, Y - d], dev(dy=d)) for d in (2, Y - 2, 1, Y - 1)}

    def relay(ref, h, first):
        out = []
        for sign, d in ((1, 2), (-1, Y - 2)):
            first[d].wait_recv()
            slot = (Y - 2 * sign) % Y
            block = ref.at[h, slot]
            if sign == (1 if h == 0 else -1):
                out.append(send(block, ref.at[h, Y // 2], dev(dy=2 * sign)))
            out.append(send(block, ref.at[h, slot - sign], dev(dy=sign)))
        return out + [first[1], first[Y - 1]]

    partners = (
        [dev(dzh=1)]
        + [dev(dy=d) for d in range(1, Y)]
        + [dev(dx=d) for d in range(1, X)]
        + [dev(dzl=d) for d in range(1, ZL)]
        + [dev(dc=1)]
        + [dev(dx=d, dzl=-d, dc=k) for d in range(1, X) for k in range(CORES)]
        + [dev(dzl=d, dc=1) for d in range(1, ZL)]
    )
    barrier = pltpu.get_barrier_semaphore()
    for partner in partners:
        pl.semaphore_signal(barrier, inc=1, device_id=partner, device_id_type=MESH)

    owner_x = lax.rem(x - zl + X, X)
    start, shift = window((lax.rem(zh + c, ZH) * X + owner_x) * group, 128)
    loads = [
        pltpu.make_async_copy(src, dst, ls.at[n])
        for n, (src, dst) in enumerate(
            (
                (w_ref, w_v),
                (kw_ref, kw_v),
                (vw_ref, vw_v),
                (hidden_ref, hidden_v),
                (gain_ref, gain_v),
                (res_ref.at[:, pl.ds(start, 512)], res_v),
                (q_ref, q_v),
                (dest_ref, dest_s),
                (off_ref, off_s),
            )
        )
    ]
    for cp in loads:
        cp.start()

    tall_rows = own32.shape[0]
    own32[...] = jnp.zeros(own32.shape, F32)
    kvl[0, 0] = jnp.zeros((tall_rows, 2 * kvw), BF16)
    loads[0].wait()
    loads[7].wait()
    loads[8].wait()
    own32[0:cw, 0:depth] = w_v[...].astype(F32)
    own32[cw : cw + 1, 0:depth] = jnp.full((1, depth), dest_s[0].astype(F32), F32)
    own32[cw + 1 : cw + 2, 0:depth] = jnp.full((1, depth), off_s[0].astype(F32), F32)
    wl = (wl_a, wl_b)
    cut = wl_a.shape[-1]
    wl_a[0, 0] = own32[:, 0:cut].astype(BF16)
    wl_b[0, 0] = own32[:, cut:].astype(BF16)
    pl.semaphore_wait(barrier, len(partners))

    w_zh = [send(w.at[0, 0], w.at[1, 0], dev(dzh=1)) for w in wl]
    right, left = {}, {}

    def begin(h, a):
        right[h, a, 1] = send(wl[a].at[h, 0], wl[a].at[h, Y - 1], dev(dy=1))
        left[h, a, 1] = send(wl[a].at[h, 0], wl[a].at[h, 1], dev(dy=-1))

    begin(0, 0)
    begin(0, 1)
    loads[1].wait()
    loads[2].wait()
    kvl[0, 0, 0:cw, 0:kvw] = kw_v[...]
    kvl[0, 0, 0:cw, kvw : 2 * kvw] = vw_v[...]
    loads[3].wait()
    act[0] = jax.nn.gelu(hidden_v[...].astype(F32)).astype(BF16)
    act_x = [send(act.at[0], act.at[X - d], dev(dx=d)) for d in FAR_X]

    loads[5].wait()
    res_t[...] = res_v[...].astype(F32).T.astype(BF16)
    shift = pl.multiple_of(shift, 16)
    res_cp = copy(res_t.at[pl.ds(shift, group)], res_in, dev(dx=-zl))

    @pl.when(zl != 0)
    def _():
        res_cp.start()

    @pl.when(zl == 0)
    def _():
        res_in[...] = res_t[pl.ds(shift, group), :]

    turn = lax.rem(group - cw * y, group)

    def columns():
        loads[4].wait()
        for h in range(ZH):
            start_g, shift_g = window((lax.rem(zh + h, ZH) * X + x) * group, 128)
            for k in range(4):
                line = gain_v[pl.ds(lax.div(start_g, 128) + k, 1), :]
                gain_t[k * 128 : (k + 1) * 128, :] = jnp.broadcast_to(line, (128, 128)).T
            turned[...] = pltpu.roll(gain_t[pl.ds(pl.multiple_of(shift_g, 16), group), :], turn, 0)
            arranged(gain_c.at[h], turned)

    def pack(h, r):
        p = ARRIVAL.index(r)
        block = wl_a[h, r].astype(F32)
        w32[h, p * cw : p * cw + cw, 0:cut] = block[0:cw, :]
        top = cw // 8 * 8
        meta[h * Y + r] = block[top : top + 8, 0:kvw]
        w32[h, p * cw : p * cw + cw, cut:depth] = wl_b[h, r].astype(F32)[0:cw, 0 : depth - cut]

    def project(lo, hi):
        acts = jnp.concatenate([act[k] for k in range(X)], axis=1)
        for h in range(ZH):
            p = jnp.dot(w32[h, lo:hi].astype(BF16), acts, preferred_element_type=F32)
            part_f[h, lo:hi] = p
            part_b[h, lo:hi] = p.astype(BF16)
        return send(part_b.at[1 - c, pl.ds(lo, hi - lo)], part_x.at[pl.ds(lo, hi - lo)], dev(dc=1))

    def scatter(lo, hi, core_cp):
        core_cp.wait_recv()
        both = part_f[c, lo:hi] + part_x[lo:hi].astype(F32)
        for k in range(X):
            blk = both[:, k * patches : (k + 1) * patches]
            half_f[k, lo:hi] = blk
            half_b[k, lo:hi] = blk.astype(BF16)
        return [
            send(
                half_b.at[lax.rem(zl + d, ZL), pl.ds(lo, hi - lo)],
                half_r.at[d - 1, pl.ds(lo, hi - lo)],
                dev(dzl=d),
            )
            for d in range(1, ZL)
        ]

    early = kvt_e.shape[-1]
    first_cut = 3 * cw // 16 * 16

    def ring(h, a, s):
        w = wl[a]
        if s < Y // 2 or h == 0:
            right[h, a, s].wait_recv()
        if s < Y // 2 - 1 or (s < Y // 2 and h == 0):
            right[h, a, s + 1] = send(w.at[h, Y - s], w.at[h, Y - s - 1], dev(dy=1))
        if s < Y // 2 or h == 1:
            left[h, a, s].wait_recv()
        if s < Y // 2 - 1 or (s < Y // 2 and h == 1):
            left[h, a, s + 1] = send(w.at[h, s], w.at[h, s + 1], dev(dy=-1))

    def finish(lo, hi, sums, pivot):
        total = half_f[zl, lo:hi] + resid[lo:hi]
        for cp in sums:
            cp.wait_recv()
        for d in range(1, ZL):
            total = total + half_r[d - 1, lo:hi].astype(F32)
        tall = total.reshape((hi - lo) // 8, 8, patches)
        once, twice = jnp.sum(tall, axis=0), jnp.sum(tall * tall, axis=0)
        if pivot is None:
            pivot = jnp.sum(once, axis=0, keepdims=True) / (hi - lo)
        normed[c, zl, lo:hi] = ((total - pivot) * gain_c[c, lo:hi]).astype(BF16)

        def block(k):
            return normed.at[c, k, pl.ds(lo, hi - lo)]

        ag = [send(block(zl), block(zl), dev(dzl=d)) for d in range(1, ZL)]
        fw = [send(block(zl), block(zl), dev(dc=1))]

        def forward(d):
            ag[d - 1].wait_recv()
            k = lax.rem(zl - d + ZL, ZL)
            fw.append(send(block(k), block(k), dev(dc=1)))

        return once, twice, pivot, fw, forward

    def exchange(ref):
        return [
            send(ref.at[0], ref.at[d * CORES + k], dev(dx=d, dzl=-d, dc=k))
            for d in range(X)
            for k in range(CORES)
            if d or k
        ]

    ring(0, 0, 1)
    ring(0, 1, 1)
    ring(0, 0, 2)
    w_zh[0].wait_recv()
    begin(1, 0)
    ring(0, 1, 2)
    w_zh[1].wait_recv()
    begin(1, 1)
    kv_zh = send(kvl.at[0, 0], kvl.at[1, 0], dev(dzh=1))
    columns()
    pack(1, 0)
    for r in (0, 1, Y - 1):
        pack(0, r)
    ring(0, 0, 3)
    ring(1, 0, 1)
    ring(0, 1, 3)
    ring(1, 1, 1)
    for r in (1, Y - 1):
        pack(1, r)
    for cp in act_x:
        cp.wait_recv()
    first_cp = project(0, first_cut)
    ring(0, 0, 4)
    ring(1, 0, 2)
    ring(0, 1, 4)
    ring(1, 1, 2)
    first_sums = scatter(0, first_cut, first_cp)
    for r in (2, Y - 2, 3, Y - 3, 4):
        pack(0, r)
    for r in (2, Y - 2):
        pack(1, r)
    second_cp = project(first_cut, early)

    @pl.when(zl != 0)
    def _():
        res_cp.wait_recv()

    turned[...] = pltpu.roll(res_in[...].astype(F32), turn, 0)
    arranged(resid, turned)
    ring(1, 0, 3)
    ring(1, 1, 3)
    second_sums = scatter(first_cut, early, second_cp)
    once_1, twice_1, here_1, fw_1, forward_1 = finish(0, first_cut, first_sums, None)
    for r in (3, Y - 3):
        pack(1, r)
    ring(1, 0, 4)
    ring(1, 1, 4)
    pack(1, 4)
    late_cp = project(early, group)

    kv_zh.wait_recv()
    kv_first = [spread(kvl, h) for h in range(ZH)]

    once_2, twice_2, here_2, fw_2, forward_2 = finish(first_cut, early, second_sums, None)
    stats_e[0] = once_1 + once_2
    st_e = exchange(stats_e)
    late_sums = scatter(early, group, late_cp)
    kv_y = [cp for h in range(ZH) for cp in relay(kvl, h, kv_first[h])]

    for cp in st_e:
        cp.wait_recv()
    sum_e = jnp.sum(jnp.sum(stats_e[...], axis=0), axis=0, keepdims=True)
    pivot = sum_e / (X * CORES * early)
    once_l, twice_l, _, fw_l, forward_l = finish(early, group, late_sums, pivot)
    stats_l[0, 0:8] = once_l
    stats_l[0, 8:16] = twice_1 + twice_2 + twice_l
    st_l = exchange(stats_l)
    scale[c, zl, 0:8] = jnp.broadcast_to(here_1 - pivot, (8, patches))
    scale[c, zl, 8:16] = jnp.broadcast_to(here_2 - pivot, (8, patches))
    sc = [
        send(scale.at[c, zl], scale.at[c, zl], dev(dzl=d, dc=k))
        for d in range(ZL)
        for k in range(CORES)
        if d or k
    ]
    for d in range(1, ZL):
        forward_1(d)
        forward_2(d)

    for cp in kv_y:
        cp.wait_recv()
    for h in range(ZH):
        for r in range(Y):
            p = ARRIVAL.index(r)
            kv32[p * cw : p * cw + cw, :] = kvl[h, r].astype(F32)[0:cw, :]
        kvt_e[h] = kv32[0:early].T.astype(BF16)
        kvt_l[h] = kv32[early:group].T.astype(BF16)
        row = lax.broadcasted_iota(jnp.int32, (early, 128), 0)
        for b, inside in enumerate((row < first_cut, row >= first_cut)):
            tilt[h, b] = jnp.dot(
                kvt_e[h],
                jnp.where(inside, gain_c[h, 0:early], 0.0).astype(BF16),
                preferred_element_type=F32,
            )
        u = lax.dot_general(
            gain_c[h].astype(BF16),
            kv32[...].astype(BF16),
            (((0,), (0,)), ((), ())),
            preferred_element_type=F32,
        )[0:8]
        weighted = u if h == 0 else weighted + u
    u_all[0] = weighted
    us = [send(u_all.at[0], u_all.at[X - d], dev(dx=d)) for d in FAR_X]

    for cp in fw_1 + fw_2 + sc:
        cp.wait_recv()
    acc = None
    for h in range(ZH):
        nt = jnp.concatenate([normed[h, k, 0:early] for k in range(X)], axis=1)
        p = jnp.dot(kvt_e[h], nt, preferred_element_type=F32)
        acc = p if acc is None else acc + p
    for k in range(X):
        part = acc[:, k * patches : (k + 1) * patches]
        for h in range(ZH):
            for b in range(2):
                part = part + tilt[h, b] * scale[h, k, 8 * b : 8 * b + 1, :]
        kv_acc[k] = part
    base = used[0]
    used[0] += X

    def kv_copy(k):
        return pltpu.make_async_remote_copy(
            src_ref=kv_s.at[k],
            dst_ref=kv_r.at[k],
            send_sem=ss.at[base + k],
            recv_sem=rs.at[base + k],
            device_id=dev(dx=k),
            device_id_type=MESH,
        )

    for d in range(ZL):
        k = lax.rem(zl - d + ZL, ZL)
        if d == 1:
            for e in range(1, ZL):
                forward_l(e)
        fw_l[d].wait_recv()
        part = kv_acc[k]
        for h in range(ZH):
            part = part + jnp.dot(
                kvt_l[h], normed[h, k, early:group], preferred_element_type=F32
            )

        @pl.when(k == 0)
        def _():
            kv_own[...] = part

        @pl.when(k != 0)
        def _():
            kv_s[k] = part.astype(BF16)
            kv_copy(k).start()

    for cp in st_l:
        cp.wait_recv()
    fin_cps = [copy(fin, fin, dev(dzl=d)) for d in range(1, ZL)]

    @pl.when(zl == 0)
    def _():
        both = jnp.sum(stats_l[...], axis=0)
        mean = (sum_e + jnp.sum(both[0:8], axis=0, keepdims=True)) / width
        var = jnp.sum(both[8:16], axis=0, keepdims=True) / width - mean * mean
        fin[0:8] = jnp.broadcast_to(lax.rsqrt(var + EPS), (8, patches))
        first_row = lax.broadcasted_iota(jnp.int32, (8, patches), 0) == 0
        fin[8:16] = jnp.where(first_row, jnp.broadcast_to(pivot - mean, (8, patches)), 0.0)
        for cp in fin_cps:
            cp.start()

    for d in range(1, ZL):

        @pl.when(zl == d)
        def _():
            fin_cps[d - 1].wait_recv()

    for cp in us:
        cp.wait_recv()
    kv = kv_own[...] + lax.dot_general(
        jnp.sum(u_all[...], axis=0),
        fin[8:16],
        (((0,), (0,)), ((), ())),
        precision=lax.Precision.HIGHEST,
        preferred_element_type=F32,
    )
    for k in range(1, X):
        kv_copy(k).wait_recv()
    for k in range(1, X):
        kv = kv + kv_r[k].astype(F32)
    kv = (kv * fin[0:1, :]).astype(BF16)

    loads[6].wait()

    def attend(n):
        kt = kv[n * HEAD_DIM : (n + 1) * HEAD_DIM, :]
        vt = kv[kvw + n * HEAD_DIM : kvw + (n + 1) * HEAD_DIM, :]
        q = q_v[:, n * HEAD_DIM : (n + 1) * HEAD_DIM]
        scores = jnp.dot(q, kt, preferred_element_type=F32) * (1.0 / HEAD_DIM**0.5)
        expo = jnp.exp(scores - jnp.max(scores, axis=1, keepdims=True))
        weights = (expo / jnp.sum(expo, axis=1, keepdims=True)).astype(BF16)
        mixed = lax.dot_general(
            weights, vt, (((1,), (1,)), ((), ())), preferred_element_type=F32
        )
        rows[n, 0, 0] = mixed.astype(BF16)
        return send(rows.at[n, 0, 0], rows.at[n, 1, 0], dev(dzh=1))

    skip = cw - cw // 8 * 8

    def masks():
        for k in range(X):
            shard = ((zh * X + lax.rem(x + k, X)) * Y + y).astype(F32)
            for s in range(MOST_IMG):
                for m in range(ZH * Y):
                    here = (meta[m, skip : skip + 1, 0:HEAD_DIM] == shard) & (
                        meta[m, skip + 1 : skip + 2, 0:HEAD_DIM] == float(s * nquery)
                    )
                    mask[(k * MOST_IMG + s) * ZH * Y + m] = jnp.broadcast_to(
                        jnp.where(here, 1.0, 0.0), (16, HEAD_DIM)
                    ).astype(BF16)

    def pick(n):
        for k in range(X):
            for s in range(MOST_IMG):
                picked = None
                for m in range(ZH * Y):
                    here = mask[(k * MOST_IMG + s) * ZH * Y + m]
                    img = rows[n, m // Y, m % Y].reshape(nquery // 16, 16, HEAD_DIM)
                    term = img * here[None]
                    picked = term if picked is None else picked + term
                slab[n, k, s * nquery : (s + 1) * nquery, :] = picked.reshape(nquery, HEAD_DIM)
        return [send(slab.at[n, d], slab_r.at[n, d - 1], dev(dx=d)) for d in FAR_X]

    r_zh, got, slabs = [], [[] for _ in range(heads)], []
    first = {}
    r_zh.append(attend(0))
    first[0, 0] = spread(rows.at[0], 0)
    for n in range(1, heads):
        r_zh.append(attend(n))
        first[n, 0] = spread(rows.at[n], 0)
    got[0] += relay(rows.at[0], 0, first[0, 0])
    for n in range(heads):
        r_zh[n].wait_recv()
        first[n, 1] = spread(rows.at[n], 1)
    for n in range(1, heads):
        got[n] += relay(rows.at[n], 0, first[n, 0])
    for n in range(heads):
        got[n] += relay(rows.at[n], 1, first[n, 1])
    masks()
    for n in range(heads):
        for cp in got[n]:
            cp.wait_recv()
        slabs.append(pick(n))
    for n in range(heads):
        for cp in slabs[n]:
            cp.wait_recv()
        result = slab[n, 0]
        for d in range(1, X):
            result = result + slab_r[n, d - 1]
        out_ref[:, n * HEAD_DIM : (n + 1) * HEAD_DIM] = result

    @pl.when(zl != 0)
    def _():
        res_cp.wait_send()

    @pl.when(zl == 0)
    def _():
        for cp in fin_cps:
            cp.wait_send()

    for k in range(1, X):
        kv_copy(k).wait_send()
    for cp in pending:
        cp.wait_send()


def local(
    vit_hidden,
    residual_stream,
    fc2_weight,
    ln_gain,
    key_weight,
    value_weight,
    query_heads,
    dest_shard,
    row_offset,
):
    patches, depth = vit_hidden.shape
    cw = fc2_weight.shape[1]
    kvw = key_weight.shape[1]
    nquery = query_heads.shape[0]
    width = residual_stream.shape[1]
    group = Y * cw
    shard_rows = MOST_IMG * nquery
    heads = kvw // HEAD_DIM
    early = 5 * cw // 16 * 16
    tall = cw // 8 * 8 + 8
    wide = (depth + 127) // 128 * 128
    cut = depth // 2 // 128 * 128 + 128
    vmem = pl.BlockSpec(memory_space=pltpu.VMEM)
    return pl.pallas_call(
        kernel,
        out_shape=pltpu.VMEM((shard_rows, kvw), BF16),
        in_specs=[pl.BlockSpec(memory_space=pl.ANY)] * 9,
        out_specs=vmem,
        scratch_shapes=[
            pltpu.VMEM((X, depth, patches), BF16),
            pltpu.VMEM((ZH, Y, tall, cut), BF16),
            pltpu.VMEM((ZH, Y, tall, wide - cut), BF16),
            pltpu.VMEM((ZH, Y, tall, 2 * kvw), BF16),
            pltpu.VMEM((tall, wide), F32),
            pltpu.VMEM((ZH * Y, 8, kvw), F32),
            pltpu.VMEM((ZH, group, depth), F32),
            pltpu.VMEM((group, 2 * kvw), F32),
            pltpu.VMEM((ZH, 2 * kvw, early), BF16),
            pltpu.VMEM((ZH, 2 * kvw, group - early), BF16),
            pltpu.VMEM((ZH, 2, 2 * kvw, patches), F32),
            pltpu.VMEM((X, 8, 2 * kvw), F32),
            pltpu.VMEM((16, patches), F32),
            pltpu.VMEM((X, 2 * kvw, patches), F32),
            pltpu.VMEM((512, 128), BF16),
            pltpu.VMEM((group, patches), BF16),
            pltpu.VMEM((group, patches), F32),
            pltpu.VMEM((group, patches), F32),
            pltpu.VMEM((512, 128), F32),
            pltpu.VMEM((ZH, group, 128), F32),
            pltpu.VMEM((ZH, group, X * patches), F32),
            pltpu.VMEM((ZH, group, X * patches), BF16),
            pltpu.VMEM((group, X * patches), BF16),
            pltpu.VMEM((X, group, patches), F32),
            pltpu.VMEM((X, group, patches), BF16),
            pltpu.VMEM((ZL - 1, group, patches), BF16),
            pltpu.VMEM((X * CORES, 8, patches), F32),
            pltpu.VMEM((X * CORES, 16, patches), F32),
            pltpu.VMEM((ZH, X, 16, patches), F32),
            pltpu.VMEM((ZH, X, group, patches), BF16),
            pltpu.VMEM((2 * kvw, patches), F32),
            pltpu.VMEM((X, 2 * kvw, patches), BF16),
            pltpu.VMEM((X, 2 * kvw, patches), BF16),
            pltpu.VMEM((heads, ZH, Y, nquery, HEAD_DIM), BF16),
            pltpu.VMEM((X * MOST_IMG * ZH * Y, 16, HEAD_DIM), BF16),
            pltpu.VMEM((heads, X, shard_rows, HEAD_DIM), BF16),
            pltpu.VMEM((heads, X - 1, shard_rows, HEAD_DIM), BF16),
            pltpu.SemaphoreType.DMA((COPIES,)),
            pltpu.SemaphoreType.DMA((COPIES,)),
            pltpu.SemaphoreType.DMA((9,)),
            pltpu.VMEM((depth, patches), BF16),
            pltpu.VMEM((patches, 512), BF16),
            pltpu.VMEM((cw, depth), BF16),
            pltpu.VMEM((width // 128, 128), F32),
            pltpu.VMEM((nquery, kvw), BF16),
            pltpu.VMEM((cw, kvw), BF16),
            pltpu.VMEM((cw, kvw), BF16),
            pltpu.SMEM((1,), jnp.int32),
            pltpu.SMEM((1,), jnp.int32),
        ],
        compiler_params=pltpu.CompilerParams(
            collective_id=0, has_side_effects=True, vmem_limit_bytes=63 * 2**20
        ),
        cost_estimate=pl.CostEstimate(
            flops=1100000000, bytes_accessed=3000000, transcendentals=200000
        ),
        name="encoder_resampler",
    )(
        vit_hidden.T,
        residual_stream,
        fc2_weight.T,
        ln_gain.reshape(width // 128, 128),
        key_weight,
        value_weight,
        query_heads,
        dest_shard,
        row_offset,
    )


def solution(mesh):
    return jax.shard_map(
        local,
        mesh=mesh,
        in_specs=(
            P("img", "tp"),
            P("img", None),
            P("tp", "img"),
            P(),
            P("img", "tp"),
            P("img", "tp"),
            P(None, "tp"),
            P("img"),
            P("img"),
        ),
        out_specs=P("img", "tp"),
        check_vma=False,
    )
```
